32 devices in a mesh: videos: 2 (over y), tm: 4 (over z), sub: 4 (over x, core).
Axes of the slice: x: 2, y: 2, z: 4, core: 2. Of those that a mesh axis runs over, the one named last changes fastest.
Arguments:
- embeddings: bfloat16 [12288, 1024], P(('videos', 'tm', 'sub')), parts along dimension 0, may hold values from -2 to 2
- offsets: int32 [12288], P(('videos', 'tm', 'sub')), parts along dimension 0, may hold values from 1 to 1024
- limits: int32 [4], P('videos'), parts along dimension 0, may hold values from 0 to 192, as said below
Outputs:
- gradient: float32 [12288, 1024], P(('videos', 'tm', 'sub')), parts along dimension 0
The draws below stay inside these ranges and needn't reach their ends.
There are 2 independent parts, one for each index of `videos`. The reference program is written for one: setup_inputs(seed, part) draws one part's arguments, and reference() takes and returns one part's arrays. A program takes and returns all parts, laid end to end along the dimension named above; each array names one. Nothing has to cross between parts.
Inputs may be any that keep to these rules, and one draw needn't show every extreme that they name: `limits`: one entry is exactly 192, less than one device's frames; the other is smaller.
All inputs are finite; a program needn't handle non-finite values.
Results may differ from the reference program's by a relative error of at most 0.0019.
Values may be sent and summed in bfloat16 or wider, within the bound.
No kernel may reach another device: no remote copies, remote signals or barrier semaphores. Data moves between devices by JAX's collectives and lax.ppermute only.
A program may use at most 64 MiB of HBM per device.

```python
import math
import jax
import jax.numpy as jnp
from jax import lax

D = 1024
BAND = 1024
ROWS = 384
FRAMES = 6144
SKIP = 192


def draw_embeddings(key, part):
    subkeys = jax.random.split(key, 16)
    two_pi = 2.0 * math.pi
    col_scale = jnp.exp(jax.random.uniform(subkeys[2], (1, D), jnp.float32, math.log(0.3), math.log(3.0)))
    rough = jnp.clip(jax.random.normal(subkeys[0], (FRAMES, D), jnp.float32), -4.0, 4.0) * col_scale / 64.0
    frame_ids = jnp.arange(FRAMES, dtype=jnp.int32)[:, None]
    drift = jnp.zeros((FRAMES, D), jnp.float32)
    for number in range(4):
        rate = jax.random.randint(subkeys[8 + number], (1, D), 164, 1093)
        phase_shift = jax.random.uniform(jax.random.fold_in(subkeys[12], number), (1, D), jnp.float32, 0.0, two_pi)
        amount = jnp.clip(jax.random.normal(jax.random.fold_in(subkeys[13], number), (1, D), jnp.float32), -3.0, 3.0)
        angle = (frame_ids * rate % 65536).astype(jnp.float32) * (two_pi / 65536.0) + phase_shift
        drift = drift + amount * jnp.cos(angle)
    drift = drift * col_scale / 64.0 * math.sqrt(0.5)
    slow_rate = jax.random.randint(subkeys[1], (), 65536 // (12 * ROWS), 65536 // (4 * ROWS) + 1)
    slow_shift = jax.random.uniform(subkeys[3], (), jnp.float32, 0.0, two_pi)
    slow_angle = (frame_ids * slow_rate % 65536).astype(jnp.float32) * (two_pi / 65536.0) + slow_shift
    level = math.log(0.12) + (math.log(0.75) - math.log(0.12)) * (0.5 + 0.5 * jnp.cos(slow_angle))
    jiggle = jax.random.uniform(subkeys[4], (FRAMES, 1), jnp.float32, math.log(0.75), math.log(1.33))
    row_scale = jnp.exp(level + jiggle)
    mixed = rough + drift
    result = mixed * row_scale
    return jnp.clip(result, -2.0, 2.0).astype(jnp.bfloat16)


def draw_limits(key, part):
    first_key, second_key = jax.random.split(key)
    which_end = jax.random.randint(first_key, (), 0, 2)
    other_end = jax.random.randint(second_key, (), 0, SKIP)
    at_most = jnp.full_like(other_end, SKIP)
    return jnp.where(which_end == 0, jnp.stack([at_most, other_end]), jnp.stack([other_end, at_most])).astype(jnp.int32)


def place_ends(drawn, key, least, high):
    dims = drawn.shape
    spot = [jax.random.randint(jax.random.fold_in(key, axis), (), 0, dims[axis]) for axis in range(len(dims))]
    drawn = drawn.at[tuple(spot)].set(least)
    longest = dims.index(max(dims))
    spot[longest] = (spot[longest] + 1) % dims[longest]
    return drawn.at[tuple(spot)].set(high)


def setup_inputs(seed: int = 0, part: int = 0) -> dict:
    streams_of = jax.random.split(jax.random.key(seed), 4)
    part_splits = jax.random.split(jax.random.fold_in(streams_of[3], part), 4)
    embeddings = draw_embeddings(jax.random.fold_in(jax.random.fold_in(streams_of[3], part), 71), part)
    offsets = place_ends(jax.random.randint(part_splits[1], (FRAMES,), 1, BAND + 1), jax.random.fold_in(part_splits[1], 1), 1, BAND).astype(jnp.int32)
    limits = draw_limits(jax.random.fold_in(jax.random.fold_in(streams_of[3], part), 71), part)
    return dict(embeddings=embeddings, offsets=offsets, limits=limits)


scale_factor = 16.0


def reference(embeddings, offsets, limits):
    frame_index = jnp.arange(FRAMES, dtype=jnp.int32)
    start_valid = limits[0]
    end_valid = FRAMES - limits[1]
    valid = (frame_index >= start_valid) & (frame_index < end_valid)
    forward = frame_index + offsets
    positive = jnp.where(forward < end_valid, forward, frame_index - offsets)
    padded = jnp.pad(embeddings, ((BAND, BAND), (0, 0)))
    zero_index = jnp.int32(0)

    def one_block(gradient, number):
        first_row = (number * ROWS).astype(jnp.int32)
        own = lax.dynamic_slice(embeddings, (first_row, zero_index), (ROWS, D))
        window = lax.dynamic_slice(padded, (first_row, zero_index), (ROWS + 2 * BAND, D))
        own_index = first_row + jnp.arange(ROWS, dtype=jnp.int32)
        win_index = first_row - BAND + jnp.arange(ROWS + 2 * BAND, dtype=jnp.int32)
        own_valid = lax.dynamic_slice(valid, (first_row,), (ROWS,))
        win_valid = (win_index >= start_valid) & (win_index < end_valid)
        own_positive = lax.dynamic_slice(positive, (first_row,), (ROWS,))
        scores = scale_factor * jnp.dot(own, window.T, preferred_element_type=jnp.float32)
        spacing = own_index[:, None] - win_index[None, :]
        in_band = (jnp.abs(spacing) <= BAND) & (spacing != 0) & own_valid[:, None] & win_valid[None, :]
        masked = jnp.where(in_band, scores, -jnp.inf)
        row_max = jnp.where(own_valid, jnp.max(masked, axis=1), jnp.float32(0.0))
        totals = jnp.sum(jnp.exp(masked - row_max[:, None]), axis=1) + jnp.where(own_valid, 0.0, 1.0)
        log_sum = row_max + jnp.log(totals)
        weights = jnp.exp(masked - log_sum[:, None])
        hits = ((win_index[None, :] == own_positive[:, None]) & own_valid[:, None]).astype(jnp.float32)
        coefficient = (weights - hits).astype(jnp.bfloat16)
        query_grad = scale_factor * jnp.dot(coefficient, window, preferred_element_type=jnp.float32)
        key_grad = scale_factor * jnp.dot(coefficient.T, own, preferred_element_type=jnp.float32)
        current = lax.dynamic_slice(gradient, (first_row, zero_index), (ROWS + 2 * BAND, D))
        current = current + key_grad
        current = current.at[BAND:BAND + ROWS].add(query_grad)
        gradient = lax.dynamic_update_slice(gradient, current, (first_row, zero_index))
        return gradient, None

    start_grad = jnp.zeros((FRAMES + 2 * BAND, D), jnp.float32)
    gradient, unused = lax.scan(one_block, start_grad, jnp.arange(FRAMES // ROWS, dtype=jnp.int32))
    return gradient[BAND:BAND + FRAMES]
```

```python
import jax
import jax.numpy as jnp
from jax import lax
from jax.sharding import PartitionSpec as P

BAND = 1024
SCALE = 16.0
AXES = ("tm", "sub")


def shift(x, count, target):
    pairs = [(i, target(i)) for i in range(count) if 0 <= target(i) < count]
    return lax.ppermute(x, AXES, pairs)


def to_core(i):
    return i ^ 1


def to_pair(i):
    return i ^ 2


def to_cross(i):
    return i + 2 if i & 2 else i - 2


def to_far(i):
    return i + 3 if i & 1 else i - 3


def to_side(i):
    return i - 2 if i & 1 else i + 2


def per_device(embeddings, offsets, limits):
    rows = embeddings.shape[0]
    count = lax.axis_size(AXES)
    assert count % 4 == 0 and lax.axis_size("sub") % 2 == 0
    tail = BAND - 2 * rows
    assert 0 < tail <= rows
    device = lax.axis_index(AXES)
    core = device % 2
    chip = (device // 2) % 2
    frames = rows * count
    start_valid = limits[0]
    end_valid = frames - limits[1]
    arange = jnp.arange(rows, dtype=jnp.int32)
    own_index = device * rows + arange
    own_valid = (own_index >= start_valid) & (own_index < end_valid)
    forward = own_index + offsets
    positive = jnp.where(forward < end_valid, forward, own_index - offsets)

    pair = shift(embeddings, count, to_pair)
    cross = shift(embeddings, count, to_cross)
    far = shift(
        jnp.where(core == 1, embeddings[rows - tail :], embeddings[:tail]), count, to_far
    )
    mate = shift(embeddings, count, to_core)
    pair_mate = shift(pair, count, to_core)
    cross_mate = shift(cross, count, to_core)

    cross_step = jnp.where(chip == 1, 2, -2)
    mate_device = device ^ 1
    blocks = [
        (embeddings, device * rows),
        (mate, mate_device * rows),
        (pair, (device ^ 2) * rows),
        (pair_mate, (mate_device ^ 2) * rows),
        (far, jnp.where(core == 1, (device + 3) * rows, (device - 2) * rows - tail)),
        (cross, (device + cross_step) * rows),
        (cross_mate, (mate_device + cross_step) * rows),
    ]
    masked = []
    indices = []
    for block, base in blocks:
        index = base + jnp.arange(block.shape[0], dtype=jnp.int32)
        valid = (index >= start_valid) & (index < end_valid)
        spacing = own_index[:, None] - index[None, :]
        inside = (jnp.abs(spacing) <= BAND) & (spacing != 0)
        inside = inside & own_valid[:, None] & valid[None, :]
        scores = SCALE * jnp.einsum(
            "td,ud->tu", embeddings, block, preferred_element_type=jnp.float32
        )
        masked.append(jnp.where(inside, scores, -jnp.inf))
        indices.append(index)
    row_max = masked[0].max(axis=1)
    for part in masked[1:]:
        row_max = jnp.maximum(row_max, part.max(axis=1))
    row_max = jnp.where(own_valid, row_max, 0.0)
    totals = jnp.where(own_valid, 0.0, 1.0)
    for part in masked:
        totals = totals + jnp.sum(jnp.exp(part - row_max[:, None]), axis=1)
    log_sum = row_max + jnp.log(totals)

    own_positive = jnp.where(own_valid, positive, -1)
    note = jnp.stack([log_sum, own_positive.astype(jnp.float32)])
    mate_note = shift(note, count, to_core)
    side = shift(jnp.stack([note, mate_note]), count, to_side)
    far_note = shift(note, count, to_far)
    side, far_note = lax.optimization_barrier((side, far_note))
    other = shift(side, count, to_core)
    far_note = jnp.where(core == 1, far_note[:, :tail], far_note[:, rows - tail :])
    swap = core == chip
    pair_note = jnp.where(swap, other[1], side[0])
    pair_mate_note = jnp.where(swap, other[0], side[1])
    cross_note = jnp.where(swap, side[0], other[1])
    cross_mate_note = jnp.where(swap, side[1], other[0])
    notes = [note, mate_note, pair_note, pair_mate_note, far_note, cross_note, cross_mate_note]

    result = jnp.zeros(embeddings.shape, jnp.float32)
    for (block, _), part, index, their in zip(blocks, masked, indices, notes):
        hits = (index[None, :] == own_positive[:, None]).astype(jnp.float32)
        out_weight = (jnp.exp(part - log_sum[:, None]) - hits).astype(jnp.bfloat16)
        result = result + jnp.einsum(
            "tu,ud->td", out_weight, block, preferred_element_type=jnp.float32
        )
    for (block, _), part, index, their in zip(blocks, masked, indices, notes):
        back_hits = (their[1].astype(jnp.int32)[None, :] == own_index[:, None]).astype(jnp.float32)
        back_weight = (jnp.exp(part - their[0][None, :]) - back_hits).astype(jnp.bfloat16)
        result = result + jnp.einsum(
            "tu,ud->td", back_weight, block, preferred_element_type=jnp.float32
        )
    return SCALE * result


def solution(mesh):
    return jax.shard_map(
        per_device,
        mesh=mesh,
        in_specs=(P(("videos", "tm", "sub"), None), P(("videos", "tm", "sub")), P("videos")),
        out_specs=P(("videos", "tm", "sub"), None),
        check_vma=False,
    )
```

```python
import functools

import jax
import jax.numpy as jnp
from jax import lax
from jax.experimental import pallas as pl
from jax.experimental.pallas import tpu as pltpu
from jax.sharding import PartitionSpec as P

BAND = 1024
SCALE = 16.0
AXES = ("tm", "sub")
NOWHERE = 1 << 29
LANES = 128
COST = 0
VMEM = pl.BlockSpec(memory_space=pltpu.VMEM)
PARAMS = pltpu.CompilerParams(vmem_limit_bytes=16 << 20)


def shift(x, count, target):
    pairs = [(i, target(i)) for i in range(count) if 0 <= target(i) < count]
    return lax.ppermute(x, AXES, pairs)


def after(x, *others):
    return lax.optimization_barrier((x, *others))[0]


def to_core(i):
    return i ^ 1


def to_pair(i):
    return i ^ 2


def to_cross(i):
    return i + 2 if i & 2 else i - 2


def to_next(i):
    return i - 4 if i & 2 else i + 4


def to_far(i):
    return i + 3 if i & 1 else i - 3


def to_side(i):
    return i - 2 if i & 1 else i + 2


def is_second(axis_index, bit):
    return lax.rem(axis_index // bit, 2)


def parts_kernel(own_ref, head_ref, rest_ref, tail_ref, sems):
    split, tail = head_ref.shape[0], tail_ref.shape[0]
    core = is_second(lax.axis_index("sub"), 1)
    first = pl.multiple_of(core * (own_ref.shape[0] - tail), 16)
    copies = [
        pltpu.make_async_copy(own_ref.at[pl.ds(0, split)], head_ref, sems.at[0]),
        pltpu.make_async_copy(own_ref.at[pl.ds(split, own_ref.shape[0] - split)], rest_ref, sems.at[1]),
        pltpu.make_async_copy(own_ref.at[pl.ds(first, tail)], tail_ref, sems.at[2]),
    ]
    for copy in copies:
        copy.start()
    for copy in copies:
        copy.wait()


def parts_of(own, split, tail):
    rows, depth = own.shape
    return pl.pallas_call(
        parts_kernel,
        out_shape=[pltpu.VMEM((size, depth), own.dtype) for size in (split, rows - split, tail)],
        in_specs=[pl.BlockSpec(memory_space=pl.ANY)],
        out_specs=[VMEM] * 3,
        scratch_shapes=[pltpu.SemaphoreType.DMA((3,))],
        compiler_params=PARAMS,
        name="parts",
    )(pltpu.with_memory_space_constraint(own, pltpu.HBM))


def score_kernel(sizes, low, first, last, *refs):
    blocks = refs[: len(sizes)]
    column_ref, row_ref = refs[len(sizes) : len(sizes) + 2]
    refs = refs[len(sizes) + 2 :]
    if first:
        own = blocks[0][...]
    else:
        own = refs[0][...]
        old_peak, old_total = refs[1][:, :1], refs[2][:, :1]
        refs = refs[3:]
    window_ref, score_ref = refs[:2]
    rows = column_ref.shape[0]
    high = low + sum(sizes)
    block = jnp.concatenate([ref[...] for ref in blocks], axis=0)
    scores = SCALE * lax.dot_general(
        own, block, (((1,), (1,)), ((), ())), preferred_element_type=jnp.float32
    )
    spacing = column_ref[...] - row_ref[:, low:high]
    inside = jnp.abs(spacing) <= BAND
    if first:
        inside = inside & (spacing != 0)
    masked = jnp.where(inside, scores, -jnp.inf)
    score_ref[...] = masked
    peak = jnp.max(masked, axis=1, keepdims=True)
    if first:
        own_valid = column_ref[...] >= 0
        peak = jnp.where(own_valid, peak, 0.0)
    else:
        peak = jnp.maximum(peak, old_peak)
    total = jnp.sum(jnp.exp(score_ref[...] - peak), axis=1, keepdims=True)
    if first:
        total = total + jnp.where(own_valid, 0.0, 1.0)
    else:
        total = total + old_total * jnp.exp(old_peak - peak)
    window_ref[...] = block
    if last:
        log_ref, note_ref = refs[2:]
        log_sum = jnp.broadcast_to(peak + jnp.log(total), (rows, LANES))
        log_ref[...] = log_sum
        note_ref[...] = log_sum.T[:1]
    else:
        peak_ref, total_ref = refs[2:]
        peak_ref[...] = jnp.broadcast_to(peak, (rows, LANES))
        total_ref[...] = jnp.broadcast_to(total, (rows, LANES))


def scores_of(low, blocks, own, column, row, state, last):
    rows, depth = own.shape
    sizes = tuple(block.shape[0] for block in blocks)
    width = sum(sizes)
    first = state is None
    wide = jax.ShapeDtypeStruct((rows, LANES), jnp.float32)
    shapes = [
        jax.ShapeDtypeStruct((width, depth), jnp.bfloat16),
        jax.ShapeDtypeStruct((rows, width), jnp.float32),
        wide,
        jax.ShapeDtypeStruct((1, rows), jnp.float32) if last else wide,
    ]
    operands = (*blocks, column, row)
    if not first:
        operands = (*operands, own, *state)
    window, scores, *state = pl.pallas_call(
        functools.partial(score_kernel, sizes, low, first, last),
        out_shape=shapes,
        in_specs=[VMEM] * len(operands),
        out_specs=[VMEM] * len(shapes),
        compiler_params=PARAMS,
        cost_estimate=pl.CostEstimate(
            flops=COST * 2 * rows * width * depth // 100, bytes_accessed=COST * width * 40, transcendentals=0
        ),
        name="scores_last" if last else ("scores_first" if first else "scores_next"),
    )(*operands)
    return window, scores, state


def product_kernel(count, split, tail, *refs):
    windows, scores = refs[:count], refs[count : 2 * count]
    column_ref, positive_ref, log_ref, row_ref, own_note, mate_note, far_note, side_ref, other_ref, out_ref = refs[2 * count :]
    rows = column_ref.shape[0]
    core = is_second(lax.axis_index("sub"), 1)
    swap = core == is_second(lax.axis_index("sub"), 2)
    pair = jnp.where(swap, other_ref[1], side_ref[0])
    pair_mate = jnp.where(swap, other_ref[0], side_ref[1])
    cross = jnp.where(swap, side_ref[0], other_ref[1])
    cross_mate = jnp.where(swap, side_ref[1], other_ref[0])
    far = jnp.where(core == 1, far_note[:, :tail], far_note[:, rows - tail :])
    notes = jnp.concatenate(
        [
            own_note[...], mate_note[...], far, pair[:, :split], pair_mate[:, :split],
            pair[:, split:], pair_mate[:, split:], cross[:, split:], cross_mate[:, split:],
            cross[:, :split], cross_mate[:, :split],
        ],
        axis=1,
    )
    log_sum, positive = log_ref[:, :1], positive_ref[...]
    frame = column_ref[...].astype(jnp.float32)
    weights = []
    low = 0
    for ref in scores:
        high = low + ref.shape[1]
        score = ref[...]
        hit = jnp.where(row_ref[:, low:high] == positive, 1.0, 0.0)
        back_hit = jnp.where(notes[1:, low:high] == frame, 1.0, 0.0)
        weight = (jnp.exp(score - log_sum) - hit) + (jnp.exp(score - notes[:1, low:high]) - back_hit)
        weights.append(weight.astype(jnp.bfloat16))
        low = high
    weights = jnp.concatenate(weights, axis=1)
    step = 256
    for low in range(0, out_ref.shape[1], step):
        block = jnp.concatenate([ref[:, low : low + step] for ref in windows], axis=0)
        out_ref[:, low : low + step] = SCALE * jnp.dot(weights, block, preferred_element_type=jnp.float32)


def product_of(windows, scores, split, tail, *extra):
    rows, depth = scores[0].shape[0], windows[0].shape[1]
    operands = (*windows, *scores, *extra)
    return pl.pallas_call(
        functools.partial(product_kernel, len(windows), split, tail),
        out_shape=jax.ShapeDtypeStruct((rows, depth), jnp.float32),
        in_specs=[VMEM] * len(operands),
        out_specs=VMEM,
        compiler_params=PARAMS,
        name="product",
    )(*operands)


def per_device(embeddings, offsets, limits):
    rows, depth = embeddings.shape
    count = lax.axis_size(AXES)
    assert count % 4 == 0 and lax.axis_size("sub") % 2 == 0
    tail = BAND - 2 * rows
    split = 2 * rows // 3
    assert 0 < tail <= rows and split % 16 == 0
    device = lax.axis_index(AXES)
    core = device % 2
    chip = (device // 2) % 2
    frames = rows * count
    start_valid = limits[0]
    end_valid = frames - limits[1]

    head, rest, tail_rows = parts_of(embeddings, split, tail)
    mate = shift(embeddings, count, to_core)
    pair_head = shift(head, count, to_pair)
    far = shift(after(tail_rows, mate), count, to_far)
    pair_rest = shift(after(rest, mate), count, to_pair)
    cross_rest = shift(after(rest, mate), count, to_cross)

    mate_device = device ^ 1
    cross = (device + jnp.where(chip == 1, 2, -2)) * rows
    cross_mate = (mate_device + jnp.where(chip == 1, 2, -2)) * rows
    far_base = jnp.where(core == 1, (device + 3) * rows, (device - 2) * rows - tail)
    pair, pair_mate = (device ^ 2) * rows, (mate_device ^ 2) * rows
    places = [
        (device * rows, rows), (mate_device * rows, rows), (far_base, tail),
        (pair, split), (pair_mate, split), (pair + split, rows - split), (pair_mate + split, rows - split),
        (cross + split, rows - split), (cross_mate + split, rows - split), (cross, split), (cross_mate, split),
    ]
    row = jnp.concatenate([base + jnp.arange(size, dtype=jnp.int32) for base, size in places])[None]
    row = jnp.where((row >= start_valid) & (row < end_valid), row, NOWHERE)
    own_index = device * rows + jnp.arange(rows, dtype=jnp.int32)
    own_valid = (own_index >= start_valid) & (own_index < end_valid)
    column = jnp.where(own_valid, own_index, -NOWHERE)[:, None]
    forward = own_index + offsets
    positive = jnp.where(forward < end_valid, forward, own_index - offsets)
    positive = jnp.where(own_valid, positive, -1)

    windows, scores = [], []

    def score(blocks, state, last=False):
        low = sum(window.shape[0] for window in windows)
        window, score, state = scores_of(low, blocks, embeddings, column, row, state, last)
        windows.append(window)
        scores.append(score)
        return state

    state = score([embeddings, mate], None)
    cross_head = shift(after(pair_head, far), count, to_next)
    pair_mate_head = shift(after(pair_head, far), count, to_core)
    state = score([far, pair_head, pair_mate_head], state)
    pair_mate_rest = shift(after(pair_rest, state[0]), count, to_core)
    cross_mate_rest = shift(cross_rest, count, to_core)
    state = score([pair_rest, pair_mate_rest, cross_rest, cross_mate_rest], state)
    cross_mate_head = shift(after(cross_head, state[0]), count, to_core)
    log_sum, log_row = score([cross_head, cross_mate_head], state, True)

    note = jnp.concatenate([log_row, positive.astype(jnp.float32)[None]])
    mate_note = shift(note, count, to_core)
    side = shift(jnp.stack([note, mate_note]), count, to_side)
    far_note = shift(note, count, to_far)
    side, far_note = lax.optimization_barrier((side, far_note))
    other = shift(side, count, to_core)
    return product_of(
        windows, scores, split, tail,
        column, positive[:, None], log_sum, row, note, mate_note, far_note, side, other,
    )


def solution(mesh):
    return jax.shard_map(
        per_device,
        mesh=mesh,
        in_specs=(P(("videos", "tm", "sub"), None), P(("videos", "tm", "sub")), P("videos")),
        out_specs=P(("videos", "tm", "sub"), None),
        check_vma=False,
    )
```

```python
import functools

import jax
import jax.numpy as jnp
from jax import lax
from jax.experimental import pallas as pl
from jax.experimental.pallas import tpu as pltpu
from jax.sharding import PartitionSpec as P

BAND = 1024
SCALE = 16.0
AXES = ("tm", "sub")
NOWHERE = 1 << 29
LANES = 128
STEP = 256
VMEM = pl.BlockSpec(memory_space=pltpu.VMEM)
COST = pl.CostEstimate(flops=0, bytes_accessed=0, transcendentals=0)
PARAMS = pltpu.CompilerParams(vmem_limit_bytes=16 << 20)


def shift(x, count, target):
    pairs = [(i, target(i)) for i in range(count) if 0 <= target(i) < count]
    return lax.ppermute(x, AXES, pairs)


def after(x, *others):
    return lax.optimization_barrier((x, *others))[0]


def to_core(i):
    return i ^ 1


def to_pair(i):
    return i ^ 2


def to_cross(i):
    return i + 2 if i & 2 else i - 2


def to_next(i):
    return i - 4 if i & 2 else i + 4


def to_far(i):
    return i + 3 if i & 1 else i - 3


def to_side(i):
    return i - 2 if i & 1 else i + 2


def is_second(axis_index, bit):
    return lax.rem(axis_index // bit, 2)


def parts_kernel(own_ref, head_ref, rest_ref, tail_ref, sems):
    split, tail = head_ref.shape[0], tail_ref.shape[0]
    core = is_second(lax.axis_index("sub"), 1)
    first = pl.multiple_of(core * (own_ref.shape[0] - tail), 16)
    copies = [
        pltpu.make_async_copy(own_ref.at[pl.ds(0, split)], head_ref, sems.at[0]),
        pltpu.make_async_copy(own_ref.at[pl.ds(split, own_ref.shape[0] - split)], rest_ref, sems.at[1]),
        pltpu.make_async_copy(own_ref.at[pl.ds(first, tail)], tail_ref, sems.at[2]),
    ]
    for copy in copies:
        copy.start()
    for copy in copies:
        copy.wait()


def parts_of(own, split, tail):
    rows, depth = own.shape
    return pl.pallas_call(
        parts_kernel,
        out_shape=[pltpu.VMEM((size, depth), own.dtype) for size in (split, rows - split, tail)],
        in_specs=[pl.BlockSpec(memory_space=pl.ANY)],
        out_specs=[VMEM] * 3,
        scratch_shapes=[pltpu.SemaphoreType.DMA((3,))],
        compiler_params=PARAMS,
        cost_estimate=COST,
        name="parts",
    )(pltpu.with_memory_space_constraint(own, pltpu.HBM))


def index_kernel(split, tail, limits_ref, offset_ref, row_ref, column_ref, positive_ref, positive_row_ref):
    rows = offset_ref.shape[1]
    device = lax.axis_index("tm") * lax.axis_size("sub") + lax.axis_index("sub")
    core, chip = is_second(device, 1), is_second(device, 2)
    start, end = limits_ref[0], lax.axis_size(AXES) * rows - limits_ref[1]
    mate = device + 1 - 2 * core
    across, step = 2 - 4 * chip, 4 * chip - 2
    far = jnp.where(core == 1, (device + 3) * rows, (device - 2) * rows - tail)
    pair, pair_mate = (device + across) * rows, (mate + across) * rows
    cross, cross_mate = (device + step) * rows, (mate + step) * rows
    places = [
        (device * rows, rows), (mate * rows, rows), (far, tail),
        (pair, split), (pair_mate, split), (pair + split, rows - split), (pair_mate + split, rows - split),
        (cross + split, rows - split), (cross_mate + split, rows - split), (cross, split), (cross_mate, split),
    ]
    low = 0
    for base, size in places:
        index = base + lax.broadcasted_iota(jnp.int32, (1, size), 1)
        index = jnp.where((index >= start) & (index < end), index, NOWHERE)
        row_ref[:, low : low + size] = index.astype(jnp.float32)
        low += size
    index = device * rows + lax.broadcasted_iota(jnp.int32, (rows, 1), 0)
    index = jnp.where((index >= start) & (index < end), index, -NOWHERE)
    column_ref[...] = index.astype(jnp.float32)
    index = device * rows + lax.broadcasted_iota(jnp.int32, (1, rows), 1)
    forward = index + offset_ref[...]
    positive = jnp.where(forward < end, forward, index - offset_ref[...])
    positive = jnp.where((index >= start) & (index < end), positive, -1).astype(jnp.float32)
    positive_row_ref[...] = positive
    positive_ref[...] = jnp.broadcast_to(positive, (LANES, rows)).T[:, :1]


def index_of(limits, offsets, split, tail, width):
    rows = offsets.shape[1]
    shapes = [(1, width), (rows, 1), (rows, 1), (1, rows)]
    return pl.pallas_call(
        functools.partial(index_kernel, split, tail),
        out_shape=[jax.ShapeDtypeStruct(shape, jnp.float32) for shape in shapes],
        in_specs=[pl.BlockSpec(memory_space=pltpu.SMEM), VMEM],
        out_specs=[VMEM] * 4,
        compiler_params=PARAMS,
        cost_estimate=COST,
        name="index",
    )(limits, offsets)


def score_kernel(sizes, low, first, last, *refs):
    blocks = refs[: len(sizes)]
    column_ref, row_ref, positive_row_ref = refs[len(sizes) : len(sizes) + 3]
    refs = refs[len(sizes) + 3 :]
    if first:
        own = blocks[0][...]
    else:
        own = refs[0][...]
        old_peak, old_total = refs[1][:, :1], refs[2][:, :1]
        refs = refs[3:]
    window_ref, score_ref = refs[:2]
    rows = column_ref.shape[0]
    high = low + sum(sizes)
    block = jnp.concatenate([ref[...] for ref in blocks], axis=0)
    scores = SCALE * lax.dot_general(
        own, block, (((1,), (1,)), ((), ())), preferred_element_type=jnp.float32
    )
    spacing = column_ref[...] - row_ref[:, low:high]
    inside = jnp.abs(spacing) <= BAND
    if first:
        inside = inside & (spacing != 0.0)
    masked = jnp.where(inside, scores, -jnp.inf)
    score_ref[...] = masked
    peak = jnp.max(masked, axis=1, keepdims=True)
    if first:
        own_valid = column_ref[...] >= 0.0
        peak = jnp.where(own_valid, peak, 0.0)
    else:
        peak = jnp.maximum(peak, old_peak)
    total = jnp.sum(jnp.exp(score_ref[...] - peak), axis=1, keepdims=True)
    if first:
        total = total + jnp.where(own_valid, 0.0, 1.0)
    else:
        total = total + old_total * jnp.exp(old_peak - peak)
    window_ref[...] = block
    if last:
        log_ref, note_ref = refs[2:]
        log_sum = jnp.broadcast_to(peak + jnp.log(total), (rows, LANES))
        log_ref[...] = log_sum
        note_ref[:1] = log_sum.T[:1]
        note_ref[1:] = positive_row_ref[...]
    else:
        peak_ref, total_ref = refs[2:]
        peak_ref[...] = jnp.broadcast_to(peak, (rows, LANES))
        total_ref[...] = jnp.broadcast_to(total, (rows, LANES))


def scores_of(low, blocks, own, column, row, positive_row, state, last):
    rows, depth = own.shape
    sizes = tuple(block.shape[0] for block in blocks)
    width = sum(sizes)
    first = state is None
    wide = jax.ShapeDtypeStruct((rows, LANES), jnp.float32)
    shapes = [
        jax.ShapeDtypeStruct((width, depth), jnp.bfloat16),
        jax.ShapeDtypeStruct((rows, width), jnp.float32),
        wide,
        jax.ShapeDtypeStruct((2, rows), jnp.float32) if last else wide,
    ]
    operands = (*blocks, column, row, positive_row)
    if not first:
        operands = (*operands, own, *state)
    window, scores, *state = pl.pallas_call(
        functools.partial(score_kernel, sizes, low, first, last),
        out_shape=shapes,
        in_specs=[VMEM] * len(operands),
        out_specs=[VMEM] * len(shapes),
        compiler_params=PARAMS,
        cost_estimate=COST,
        name="scores_last" if last else ("scores_first" if first else "scores_next"),
    )(*operands)
    return window, scores, state


def weight_of(score, log_sum, index, wanted):
    weight = jnp.exp(score - log_sum) - jnp.where(index == wanted, 1.0, 0.0)
    return weight.astype(jnp.bfloat16)


def product_out_kernel(count, *refs):
    windows, scores = refs[:count], refs[count : 2 * count]
    column_ref, positive_ref, log_ref, row_ref, own_note, mate_note, out_ref = refs[2 * count :]
    log_sum, positive = log_ref[:, :1], positive_ref[...]
    weights = []
    low = 0
    for ref in scores:
        high = low + ref.shape[1]
        weights.append(weight_of(ref[...], log_sum, row_ref[:, low:high], positive))
        low = high
    notes = jnp.concatenate([own_note[...], mate_note[...]], axis=1)
    weights.append(weight_of(scores[0][...], notes[:1], notes[1:], column_ref[...]))
    weights = jnp.concatenate(weights, axis=1)
    for low in range(0, out_ref.shape[1], STEP):
        block = jnp.concatenate([ref[:, low : low + STEP] for ref in (*windows, windows[0])], axis=0)
        out_ref[:, low : low + STEP] = jnp.dot(weights, block, preferred_element_type=jnp.float32)


def product_back_kernel(count, split, tail, *refs):
    windows, scores = refs[:count], refs[count : 2 * count]
    column_ref, far_note, side_ref, other_ref, base_ref, out_ref, held_ref, sems = refs[2 * count :]
    rows = column_ref.shape[0]
    core = is_second(lax.axis_index("sub"), 1)
    swap = core == is_second(lax.axis_index("sub"), 2)
    pair = jnp.where(swap, other_ref[1], side_ref[0])
    pair_mate = jnp.where(swap, other_ref[0], side_ref[1])
    cross = jnp.where(swap, side_ref[0], other_ref[1])
    cross_mate = jnp.where(swap, side_ref[1], other_ref[0])
    far = jnp.where(core == 1, far_note[:, :tail], far_note[:, rows - tail :])
    notes = jnp.concatenate(
        [
            far, pair[:, :split], pair_mate[:, :split], pair[:, split:], pair_mate[:, split:],
            cross[:, split:], cross_mate[:, split:], cross[:, :split], cross_mate[:, :split],
        ],
        axis=1,
    )
    weights = []
    low = 0
    for ref in scores:
        high = low + ref.shape[1]
        weights.append(weight_of(ref[...], notes[:1, low:high], notes[1:, low:high], column_ref[...]))
        low = high
    weights = jnp.concatenate(weights, axis=1)
    copies = []
    for number, low in enumerate(range(0, out_ref.shape[1], STEP)):
        place = pl.ds(low, STEP)
        block = jnp.concatenate([ref[:, low : low + STEP] for ref in windows], axis=0)
        part = jnp.dot(weights, block, preferred_element_type=jnp.float32)
        held_ref[:, low : low + STEP] = SCALE * (part + base_ref[:, low : low + STEP])
        copies.append(pltpu.make_async_copy(held_ref.at[:, place], out_ref.at[:, place], sems.at[number]))
        copies[-1].start()
    for copy in copies:
        copy.wait()


def product_of(kernel, operands, scratch, place, name):
    rows, depth = operands[-1].shape if scratch else (operands[-1].shape[1], operands[0].shape[1])
    return pl.pallas_call(
        kernel,
        out_shape=jax.ShapeDtypeStruct((rows, depth), jnp.float32),
        in_specs=[VMEM] * len(operands),
        out_specs=place,
        scratch_shapes=scratch,
        compiler_params=PARAMS,
        cost_estimate=COST,
        name=name,
    )(*operands)


def per_device(embeddings, offsets, limits):
    rows, depth = embeddings.shape
    count = lax.axis_size(AXES)
    assert count % 4 == 0 and lax.axis_size("sub") % 4 == 0
    tail = BAND - 2 * rows
    split = 2 * rows // 3
    assert 0 < tail <= rows and split % 16 == 0

    head, rest, tail_rows = parts_of(embeddings, split, tail)
    mate = shift(embeddings, count, to_core)
    pair_head = shift(head, count, to_pair)
    far = shift(after(tail_rows, mate), count, to_far)
    row, column, positive, positive_row = index_of(
        limits, offsets[None], split, tail, 6 * rows + tail
    )

    windows, scores = [], []

    def score(blocks, state, last=False):
        low = sum(window.shape[0] for window in windows)
        window, score, state = scores_of(low, blocks, embeddings, column, row, positive_row, state, last)
        windows.append(window)
        scores.append(score)
        return state

    state = score([embeddings, mate], None)
    pair_rest = shift(after(rest, state[0]), count, to_pair)
    pair_mate_head = shift(after(pair_head, far, state[0]), count, to_core)
    cross_rest = shift(after(rest, pair_head, far), count, to_cross)
    cross_head = shift(after(pair_head, far, state[0]), count, to_next)
    pair_mate_rest = shift(pair_rest, count, to_core)
    state = score([far, pair_head, pair_mate_head, pair_rest, pair_mate_rest], state)
    cross_mate_rest = shift(cross_rest, count, to_core)
    cross_mate_head = shift(after(cross_head, state[0]), count, to_core)
    log_sum, note = score([cross_rest, cross_mate_rest, cross_head, cross_mate_head], state, True)

    mate_note = shift(note, count, to_core)
    side = shift(jnp.stack([note, mate_note]), count, to_side)
    far_note = shift(note, count, to_far)
    base = product_of(
        functools.partial(product_out_kernel, len(windows)),
        (*windows, *scores, column, positive, log_sum, row, note, mate_note),
        [], VMEM, "product_out",
    )
    side, far_note, base = lax.optimization_barrier((side, far_note, base))
    other = shift(side, count, to_core)
    return product_of(
        functools.partial(product_back_kernel, len(windows) - 1, split, tail),
        (*windows[1:], *scores[1:], column, far_note, side, other, base),
        [pltpu.VMEM((rows, depth), jnp.float32), pltpu.SemaphoreType.DMA((depth // STEP,))],
        pl.BlockSpec(memory_space=pl.ANY), "product_back",
    )


def solution(mesh):
    return jax.shard_map(
        per_device,
        mesh=mesh,
        in_specs=(P(("videos", "tm", "sub"), None), P(("videos", "tm", "sub")), P("videos")),
        out_specs=P(("videos", "tm", "sub"), None),
        check_vma=False,
    )
```

```python
import functools

import jax
import jax.numpy as jnp
from jax import lax
from jax.experimental import pallas as pl
from jax.experimental.pallas import tpu as pltpu
from jax.sharding import PartitionSpec as P

BAND = 1024
SCALE = 16.0
AXES = ("tm", "sub")
NOWHERE = 1 << 29
LANES = 128
STEP = 256
VMEM = pl.BlockSpec(memory_space=pltpu.VMEM)
COST = pl.CostEstimate(flops=0, bytes_accessed=0, transcendentals=0)
PARAMS = pltpu.CompilerParams(vmem_limit_bytes=16 << 20)


def shift(x, count, target):
    pairs = [(i, target(i)) for i in range(count) if 0 <= target(i) < count]
    return lax.ppermute(x, AXES, pairs)


def after(x, *others):
    return lax.optimization_barrier((x, *others))[0]


def to_core(i):
    return i ^ 1


def to_pair(i):
    return i ^ 2


def to_cross(i):
    return i + 2 if i & 2 else i - 2


def to_next(i):
    return i - 4 if i & 2 else i + 4


def to_far(i):
    return i + 3 if i & 1 else i - 3


def is_second(axis_index, bit):
    return lax.rem(axis_index // bit, 2)


def parts_kernel(own_ref, head_ref, rest_ref, tail_ref, sems):
    split, tail = head_ref.shape[0], tail_ref.shape[0]
    core = is_second(lax.axis_index("sub"), 1)
    first = pl.multiple_of(core * (own_ref.shape[0] - tail), 16)
    copies = [
        pltpu.make_async_copy(own_ref.at[pl.ds(0, split)], head_ref, sems.at[0]),
        pltpu.make_async_copy(own_ref.at[pl.ds(split, own_ref.shape[0] - split)], rest_ref, sems.at[1]),
        pltpu.make_async_copy(own_ref.at[pl.ds(first, tail)], tail_ref, sems.at[2]),
    ]
    for copy in copies:
        copy.start()
    for copy in copies:
        copy.wait()


def parts_of(own, split, tail):
    rows, depth = own.shape
    return pl.pallas_call(
        parts_kernel,
        out_shape=[pltpu.VMEM((size, depth), own.dtype) for size in (split, rows - split, tail)],
        in_specs=[pl.BlockSpec(memory_space=pl.ANY)],
        out_specs=[VMEM] * 3,
        scratch_shapes=[pltpu.SemaphoreType.DMA((3,))],
        compiler_params=PARAMS,
        cost_estimate=COST,
        name="parts",
    )(pltpu.with_memory_space_constraint(own, pltpu.HBM))


def index_kernel(split, tail, limits_ref, offset_ref, row_ref, column_ref, positive_ref, positive_row_ref):
    rows = offset_ref.shape[1]
    device = lax.axis_index("tm") * lax.axis_size("sub") + lax.axis_index("sub")
    core, chip = is_second(device, 1), is_second(device, 2)
    start, end = limits_ref[0], lax.axis_size(AXES) * rows - limits_ref[1]
    mate = device + 1 - 2 * core
    across, step = 2 - 4 * chip, 4 * chip - 2
    far = jnp.where(core == 1, (device + 3) * rows, (device - 2) * rows - tail)
    pair, pair_mate = (device + across) * rows, (mate + across) * rows
    cross, cross_mate = (device + step) * rows, (mate + step) * rows
    places = [
        (device * rows, rows), (mate * rows, rows), (far, tail),
        (pair, split), (pair_mate, split), (pair + split, rows - split), (pair_mate + split, rows - split),
        (cross + split, rows - split), (cross_mate + split, rows - split), (cross, split), (cross_mate, split),
    ]
    low = 0
    for base, size in places:
        index = base + lax.broadcasted_iota(jnp.int32, (1, size), 1)
        index = jnp.where((index >= start) & (index < end), index, NOWHERE)
        row_ref[:, low : low + size] = index.astype(jnp.float32)
        low += size
    index = device * rows + lax.broadcasted_iota(jnp.int32, (rows, 1), 0)
    index = jnp.where((index >= start) & (index < end), index, -NOWHERE)
    column_ref[...] = index.astype(jnp.float32)
    index = device * rows + lax.broadcasted_iota(jnp.int32, (1, rows), 1)
    forward = index + offset_ref[...]
    positive = jnp.where(forward < end, forward, index - offset_ref[...])
    positive = jnp.where((index >= start) & (index < end), positive, -1).astype(jnp.float32)
    positive_row_ref[...] = positive
    positive_ref[...] = jnp.broadcast_to(positive, (LANES, rows)).T[:, :1]


def index_of(limits, offsets, split, tail, width):
    rows = offsets.shape[1]
    shapes = [(1, width), (rows, 1), (rows, 1), (1, rows)]
    return pl.pallas_call(
        functools.partial(index_kernel, split, tail),
        out_shape=[jax.ShapeDtypeStruct(shape, jnp.float32) for shape in shapes],
        in_specs=[pl.BlockSpec(memory_space=pltpu.SMEM), VMEM],
        out_specs=[VMEM] * 4,
        compiler_params=PARAMS,
        cost_estimate=COST,
        name="index",
    )(limits, offsets)


def score_kernel(sizes, low, first, last, *refs):
    blocks = refs[: len(sizes)]
    column_ref, row_ref, positive_row_ref = refs[len(sizes) : len(sizes) + 3]
    refs = refs[len(sizes) + 3 :]
    if first:
        own = blocks[0][...]
    else:
        own = refs[0][...]
        old_peak, old_total = refs[1][:, :1], refs[2][:, :1]
        refs = refs[3:]
    window_ref, score_ref = refs[:2]
    rows = column_ref.shape[0]
    high = low + sum(sizes)
    block = jnp.concatenate([ref[...] for ref in blocks], axis=0)
    scores = SCALE * lax.dot_general(
        own, block, (((1,), (1,)), ((), ())), preferred_element_type=jnp.float32
    )
    spacing = column_ref[...] - row_ref[:, low:high]
    inside = jnp.abs(spacing) <= BAND
    if first:
        inside = inside & (spacing != 0.0)
    masked = jnp.where(inside, scores, -jnp.inf)
    score_ref[...] = masked
    peak = jnp.max(masked, axis=1, keepdims=True)
    if first:
        own_valid = column_ref[...] >= 0.0
        peak = jnp.where(own_valid, peak, 0.0)
    else:
        peak = jnp.maximum(peak, old_peak)
    total = jnp.sum(jnp.exp(score_ref[...] - peak), axis=1, keepdims=True)
    if first:
        total = total + jnp.where(own_valid, 0.0, 1.0)
    else:
        total = total + old_total * jnp.exp(old_peak - peak)
    window_ref[...] = block
    if last:
        log_ref, note_ref = refs[2:]
        log_sum = jnp.broadcast_to(peak + jnp.log(total), (rows, LANES))
        log_ref[...] = log_sum
        note_ref[:1] = log_sum.T[:1]
        note_ref[1:] = positive_row_ref[...]
    else:
        peak_ref, total_ref = refs[2:]
        peak_ref[...] = jnp.broadcast_to(peak, (rows, LANES))
        total_ref[...] = jnp.broadcast_to(total, (rows, LANES))


def scores_of(low, blocks, own, column, row, positive_row, state, last):
    rows, depth = own.shape
    sizes = tuple(block.shape[0] for block in blocks)
    width = sum(sizes)
    first = state is None
    wide = jax.ShapeDtypeStruct((rows, LANES), jnp.float32)
    shapes = [
        jax.ShapeDtypeStruct((width, depth), jnp.bfloat16),
        jax.ShapeDtypeStruct((rows, width), jnp.float32),
        wide,
        jax.ShapeDtypeStruct((2, rows), jnp.float32) if last else wide,
    ]
    operands = (*blocks, column, row, positive_row)
    if not first:
        operands = (*operands, own, *state)
    window, scores, *state = pl.pallas_call(
        functools.partial(score_kernel, sizes, low, first, last),
        out_shape=shapes,
        in_specs=[VMEM] * len(operands),
        out_specs=[VMEM] * len(shapes),
        compiler_params=PARAMS,
        cost_estimate=COST,
        name="scores_last" if last else ("scores_first" if first else "scores_next"),
    )(*operands)
    return window, scores, state


def weight_of(score, log_sum, index, wanted):
    weight = jnp.exp(score - log_sum) - jnp.where(index == wanted, 1.0, 0.0)
    return weight.astype(jnp.bfloat16)


def product_out_kernel(count, *refs):
    windows, scores = refs[:count], refs[count : 2 * count]
    column_ref, positive_ref, log_ref, row_ref, own_note, mate_note, out_ref = refs[2 * count :]
    log_sum, positive = log_ref[:, :1], positive_ref[...]
    weights = []
    low = 0
    for ref in scores:
        high = low + ref.shape[1]
        weights.append(weight_of(ref[...], log_sum, row_ref[:, low:high], positive))
        low = high
    notes = jnp.concatenate([own_note[...], mate_note[...]], axis=1)
    weights.append(weight_of(scores[0][...], notes[:1], notes[1:], column_ref[...]))
    weights = jnp.concatenate(weights, axis=1)
    for low in range(0, out_ref.shape[1], STEP):
        block = jnp.concatenate([ref[:, low : low + STEP] for ref in (*windows, windows[0])], axis=0)
        out_ref[:, low : low + STEP] = jnp.dot(weights, block, preferred_element_type=jnp.float32)


def product_back_kernel(count, split, tail, *refs):
    windows, scores = refs[:count], refs[count : 2 * count]
    column_ref, far_note, pair_ref, cross_ref, other_ref, base_ref, out_ref, held_ref, sems = refs[2 * count :]
    rows = column_ref.shape[0]
    core = is_second(lax.axis_index("sub"), 1)
    pair, cross = pair_ref[...], cross_ref[...]
    pair_mate, cross_mate = other_ref[0], other_ref[1]
    far = jnp.where(core == 1, far_note[:, :tail], far_note[:, rows - tail :])
    notes = jnp.concatenate(
        [
            far, pair[:, :split], pair_mate[:, :split], pair[:, split:], pair_mate[:, split:],
            cross[:, split:], cross_mate[:, split:], cross[:, :split], cross_mate[:, :split],
        ],
        axis=1,
    )
    weights = []
    low = 0
    for ref in scores:
        high = low + ref.shape[1]
        weights.append(weight_of(ref[...], notes[:1, low:high], notes[1:, low:high], column_ref[...]))
        low = high
    weights = jnp.concatenate(weights, axis=1)
    copies = []
    for number, low in enumerate(range(0, out_ref.shape[1], STEP)):
        place = pl.ds(low, STEP)
        block = jnp.concatenate([ref[:, low : low + STEP] for ref in windows], axis=0)
        part = jnp.dot(weights, block, preferred_element_type=jnp.float32)
        held_ref[:, low : low + STEP] = SCALE * (part + base_ref[:, low : low + STEP])
        copies.append(pltpu.make_async_copy(held_ref.at[:, place], out_ref.at[:, place], sems.at[number]))
        copies[-1].start()
    for copy in copies:
        copy.wait()


def product_of(kernel, operands, scratch, place, name):
    rows, depth = operands[-1].shape if scratch else (operands[-1].shape[1], operands[0].shape[1])
    return pl.pallas_call(
        kernel,
        out_shape=jax.ShapeDtypeStruct((rows, depth), jnp.float32),
        in_specs=[VMEM] * len(operands),
        out_specs=place,
        scratch_shapes=scratch,
        compiler_params=PARAMS,
        cost_estimate=COST,
        name=name,
    )(*operands)


def per_device(embeddings, offsets, limits):
    rows, depth = embeddings.shape
    count = lax.axis_size(AXES)
    assert count % 4 == 0 and lax.axis_size("sub") % 4 == 0
    tail = BAND - 2 * rows
    split = 2 * rows // 3
    assert 0 < tail <= rows and split % 16 == 0

    head, rest, tail_rows = parts_of(embeddings, split, tail)
    mate = shift(embeddings, count, to_core)
    pair_head = shift(head, count, to_pair)
    far = shift(after(tail_rows, mate), count, to_far)
    row, column, positive, positive_row = index_of(
        limits, offsets[None], split, tail, 6 * rows + tail
    )

    windows, scores = [], []

    def score(blocks, state, last=False):
        low = sum(window.shape[0] for window in windows)
        window, score, state = scores_of(low, blocks, embeddings, column, row, positive_row, state, last)
        windows.append(window)
        scores.append(score)
        return state

    state = score([embeddings, mate], None)
    pair_rest = shift(after(rest, state[0]), count, to_pair)
    pair_mate_head = shift(after(pair_head, far, state[0]), count, to_core)
    cross_rest = shift(after(rest, pair_head, far), count, to_cross)
    cross_head = shift(after(pair_head, far, state[0]), count, to_next)
    pair_mate_rest = shift(pair_rest, count, to_core)
    state = score([far, pair_head, pair_mate_head, pair_rest, pair_mate_rest], state)
    cross_mate_rest = shift(cross_rest, count, to_core)
    cross_mate_head = shift(after(cross_head, state[0]), count, to_core)
    log_sum, note = score([cross_rest, cross_mate_rest, cross_head, cross_mate_head], state, True)

    mate_note = shift(note, count, to_core)
    pair_note = shift(note, count, to_pair)
    far_note = shift(note, count, to_far)
    cross_note = shift(pair_note, count, to_next)
    base = product_of(
        functools.partial(product_out_kernel, len(windows)),
        (*windows, *scores, column, positive, log_sum, row, note, mate_note),
        [], VMEM, "product_out",
    )
    cross_note, far_note, base = lax.optimization_barrier((cross_note, far_note, base))
    other = shift(jnp.stack([pair_note, cross_note]), count, to_core)
    return product_of(
        functools.partial(product_back_kernel, len(windows) - 1, split, tail),
        (*windows[1:], *scores[1:], column, far_note, pair_note, cross_note, other, base),
        [pltpu.VMEM((rows, depth), jnp.float32), pltpu.SemaphoreType.DMA((depth // STEP,))],
        pl.BlockSpec(memory_space=pl.ANY), "product_back",
    )


def solution(mesh):
    return jax.shard_map(
        per_device,
        mesh=mesh,
        in_specs=(P(("videos", "tm", "sub"), None), P(("videos", "tm", "sub")), P("videos")),
        out_specs=P(("videos", "tm", "sub"), None),
        check_vma=False,
    )
```

```python
import functools

import jax
import jax.numpy as jnp
from jax import lax
from jax.experimental import pallas as pl
from jax.experimental.pallas import tpu as pltpu
from jax.sharding import PartitionSpec as P

BAND = 1024
SCALE = 16.0
AXES = ("tm", "sub")
NOWHERE = 1 << 29
LANES = 128
STEP = 256
VMEM = pl.BlockSpec(memory_space=pltpu.VMEM)
COST = pl.CostEstimate(flops=0, bytes_accessed=0, transcendentals=0)
PARAMS = pltpu.CompilerParams(vmem_limit_bytes=16 << 20)


def shift(x, count, target):
    pairs = [(i, target(i)) for i in range(count) if 0 <= target(i) < count]
    return lax.ppermute(x, AXES, pairs)


def after(x, *others):
    return lax.optimization_barrier((x, *others))[0]


def to_core(i):
    return i ^ 1


def to_pair(i):
    return i ^ 2


def to_cross(i):
    return i + 2 if i & 2 else i - 2


def to_next(i):
    return i - 4 if i & 2 else i + 4


def to_far(i):
    return i + 3 if i & 1 else i - 3


def is_second(axis_index, bit):
    return lax.rem(axis_index // bit, 2)


def head_kernel(own_ref, head_ref, sem):
    copy = pltpu.make_async_copy(own_ref.at[pl.ds(0, head_ref.shape[0])], head_ref, sem)
    copy.start()
    copy.wait()


def parts_kernel(own_ref, rest_ref, tail_ref, sems):
    rest, tail = rest_ref.shape[0], tail_ref.shape[0]
    core = is_second(lax.axis_index("sub"), 1)
    first = pl.multiple_of(core * (own_ref.shape[0] - tail), 16)
    copies = [
        pltpu.make_async_copy(own_ref.at[pl.ds(own_ref.shape[0] - rest, rest)], rest_ref, sems.at[0]),
        pltpu.make_async_copy(own_ref.at[pl.ds(first, tail)], tail_ref, sems.at[1]),
    ]
    for copy in copies:
        copy.start()
    for copy in copies:
        copy.wait()


def copies_of(kernel, own, sizes, semaphores, name):
    return pl.pallas_call(
        kernel,
        out_shape=[pltpu.VMEM((size, own.shape[1]), own.dtype) for size in sizes],
        in_specs=[pl.BlockSpec(memory_space=pl.ANY)],
        out_specs=[VMEM] * len(sizes),
        scratch_shapes=[semaphores],
        compiler_params=PARAMS,
        cost_estimate=COST,
        name=name,
    )(pltpu.with_memory_space_constraint(own, pltpu.HBM))


def index_kernel(split, tail, limits_ref, offset_ref, row_ref, column_ref, positive_ref, positive_row_ref):
    rows = offset_ref.shape[1]
    device = lax.axis_index("tm") * lax.axis_size("sub") + lax.axis_index("sub")
    core, chip = is_second(device, 1), is_second(device, 2)
    start, end = limits_ref[0], lax.axis_size(AXES) * rows - limits_ref[1]
    mate = device + 1 - 2 * core
    across, step = 2 - 4 * chip, 4 * chip - 2
    far = jnp.where(core == 1, (device + 3) * rows, (device - 2) * rows - tail)
    pair, pair_mate = (device + across) * rows, (mate + across) * rows
    cross, cross_mate = (device + step) * rows, (mate + step) * rows
    places = [
        (device * rows, rows), (mate * rows, rows), (far, tail),
        (pair, split), (pair_mate, split), (pair + split, rows - split), (pair_mate + split, rows - split),
        (cross + split, rows - split), (cross_mate + split, rows - split), (cross, split), (cross_mate, split),
    ]
    low = 0
    for base, size in places:
        index = base + lax.broadcasted_iota(jnp.int32, (1, size), 1)
        index = jnp.where((index >= start) & (index < end), index, NOWHERE)
        row_ref[:, low : low + size] = index.astype(jnp.float32)
        low += size
    index = device * rows + lax.broadcasted_iota(jnp.int32, (rows, 1), 0)
    index = jnp.where((index >= start) & (index < end), index, -NOWHERE)
    column_ref[...] = index.astype(jnp.float32)
    index = device * rows + lax.broadcasted_iota(jnp.int32, (1, rows), 1)
    forward = index + offset_ref[...]
    positive = jnp.where(forward < end, forward, index - offset_ref[...])
    positive = jnp.where((index >= start) & (index < end), positive, -1).astype(jnp.float32)
    positive_row_ref[...] = positive
    positive_ref[...] = jnp.broadcast_to(positive, (LANES, rows)).T[:, :1]


def index_of(limits, offsets, split, tail, width):
    rows = offsets.shape[1]
    shapes = [(1, width), (rows, 1), (rows, 1), (1, rows)]
    return pl.pallas_call(
        functools.partial(index_kernel, split, tail),
        out_shape=[jax.ShapeDtypeStruct(shape, jnp.float32) for shape in shapes],
        in_specs=[pl.BlockSpec(memory_space=pltpu.SMEM), VMEM],
        out_specs=[VMEM] * 4,
        compiler_params=PARAMS,
        cost_estimate=COST,
        name="index",
    )(limits, offsets)


def score_kernel(sizes, low, first, last, *refs):
    blocks = refs[: len(sizes)]
    column_ref, row_ref, positive_row_ref = refs[len(sizes) : len(sizes) + 3]
    refs = refs[len(sizes) + 3 :]
    if first:
        own = blocks[0][...]
    else:
        own = refs[0][...]
        old_peak, old_total = refs[1][:, :1], refs[2][:, :1]
        refs = refs[3:]
    window_ref, score_ref = refs[:2]
    rows = column_ref.shape[0]
    high = low + sum(sizes)
    block = jnp.concatenate([ref[...] for ref in blocks], axis=0)
    scores = SCALE * lax.dot_general(
        own, block, (((1,), (1,)), ((), ())), preferred_element_type=jnp.float32
    )
    spacing = column_ref[...] - row_ref[:, low:high]
    inside = jnp.abs(spacing) <= BAND
    if first:
        inside = inside & (spacing != 0.0)
    masked = jnp.where(inside, scores, -jnp.inf)
    score_ref[...] = masked
    peak = jnp.max(masked, axis=1, keepdims=True)
    if first:
        own_valid = column_ref[...] >= 0.0
        peak = jnp.where(own_valid, peak, 0.0)
    else:
        peak = jnp.maximum(peak, old_peak)
    total = jnp.sum(jnp.exp(score_ref[...] - peak), axis=1, keepdims=True)
    if first:
        total = total + jnp.where(own_valid, 0.0, 1.0)
    else:
        total = total + old_total * jnp.exp(old_peak - peak)
    window_ref[...] = block
    if last:
        log_ref, note_ref = refs[2:]
        log_sum = jnp.broadcast_to(peak + jnp.log(total), (rows, LANES))
        log_ref[...] = log_sum
        note_ref[:1] = log_sum.T[:1]
        note_ref[1:] = positive_row_ref[...]
    else:
        peak_ref, total_ref = refs[2:]
        peak_ref[...] = jnp.broadcast_to(peak, (rows, LANES))
        total_ref[...] = jnp.broadcast_to(total, (rows, LANES))


def scores_of(low, blocks, own, column, row, positive_row, state, last):
    rows, depth = own.shape
    sizes = tuple(block.shape[0] for block in blocks)
    width = sum(sizes)
    first = state is None
    wide = jax.ShapeDtypeStruct((rows, LANES), jnp.float32)
    shapes = [
        jax.ShapeDtypeStruct((width, depth), jnp.bfloat16),
        jax.ShapeDtypeStruct((rows, width), jnp.float32),
        wide,
        jax.ShapeDtypeStruct((2, rows), jnp.float32) if last else wide,
    ]
    operands = (*blocks, column, row, positive_row)
    if not first:
        operands = (*operands, own, *state)
    window, scores, *state = pl.pallas_call(
        functools.partial(score_kernel, sizes, low, first, last),
        out_shape=shapes,
        in_specs=[VMEM] * len(operands),
        out_specs=[VMEM] * len(shapes),
        compiler_params=PARAMS,
        cost_estimate=COST,
        name="scores_last" if last else ("scores_first" if first else "scores_next"),
    )(*operands)
    return window, scores, state


def weight_of(score, log_sum, index, wanted):
    weight = jnp.exp(score - log_sum) - jnp.where(index == wanted, 1.0, 0.0)
    return weight.astype(jnp.bfloat16)


def product_out_kernel(count, split, tail, *refs):
    windows, scores = refs[:count], refs[count : 2 * count]
    column_ref, positive_ref, log_ref, row_ref, own_note, mate_note, pair_note, out_ref = refs[2 * count :]
    log_sum, positive = log_ref[:, :1], positive_ref[...]
    weights = []
    low = 0
    for ref in scores:
        high = low + ref.shape[1]
        weights.append(weight_of(ref[...], log_sum, row_ref[:, low:high], positive))
        low = high
    notes = jnp.concatenate([own_note[...], mate_note[...]], axis=1)
    weights.append(weight_of(scores[0][...], notes[:1], notes[1:], column_ref[...]))
    weights.append(
        weight_of(scores[1][:, tail : tail + split], pair_note[:1, :split], pair_note[1:, :split], column_ref[...])
    )
    weights = jnp.concatenate(weights, axis=1)
    for low in range(0, out_ref.shape[1], STEP):
        place = slice(low, low + STEP)
        blocks = [ref[:, place] for ref in (*windows, windows[0])] + [windows[1][tail : tail + split, place]]
        block = jnp.concatenate(blocks, axis=0)
        out_ref[:, low : low + STEP] = jnp.dot(weights, block, preferred_element_type=jnp.float32)


def product_back_kernel(count, split, tail, *refs):
    windows, scores = refs[:count], refs[count : 2 * count]
    column_ref, far_note, pair_ref, cross_ref, other_ref, base_ref, out_ref, held_ref, sems = refs[2 * count :]
    rows = column_ref.shape[0]
    core = is_second(lax.axis_index("sub"), 1)
    pair, cross = pair_ref[...], cross_ref[...]
    pair_mate, cross_mate = other_ref[0], other_ref[1]
    far = jnp.where(core == 1, far_note[:, :tail], far_note[:, rows - tail :])
    notes = jnp.concatenate(
        [
            far, pair_mate[:, :split], pair[:, split:], pair_mate[:, split:],
            cross[:, split:], cross_mate[:, split:], cross[:, :split], cross_mate[:, :split],
        ],
        axis=1,
    )
    weights = []
    low = 0
    for number, ref in enumerate(scores):
        score = ref[...]
        if number == 0:
            score = jnp.concatenate([score[:, :tail], score[:, tail + split :]], axis=1)
        high = low + score.shape[1]
        weights.append(weight_of(score, notes[:1, low:high], notes[1:, low:high], column_ref[...]))
        low = high
    weights = jnp.concatenate(weights, axis=1)
    copies = []
    for number, low in enumerate(range(0, out_ref.shape[1], STEP)):
        place = pl.ds(low, STEP)
        first = windows[0][:, low : low + STEP]
        blocks = [first[:tail], first[tail + split :]] + [ref[:, low : low + STEP] for ref in windows[1:]]
        block = jnp.concatenate(blocks, axis=0)
        part = jnp.dot(weights, block, preferred_element_type=jnp.float32)
        held_ref[:, low : low + STEP] = SCALE * (part + base_ref[:, low : low + STEP])
        copies.append(pltpu.make_async_copy(held_ref.at[:, place], out_ref.at[:, place], sems.at[number]))
        copies[-1].start()
    for copy in copies:
        copy.wait()


def product_of(kernel, operands, scratch, place, name):
    rows, depth = operands[-1].shape if scratch else (operands[-1].shape[1], operands[0].shape[1])
    return pl.pallas_call(
        kernel,
        out_shape=jax.ShapeDtypeStruct((rows, depth), jnp.float32),
        in_specs=[VMEM] * len(operands),
        out_specs=place,
        scratch_shapes=scratch,
        compiler_params=PARAMS,
        cost_estimate=COST,
        name=name,
    )(*operands)


def per_device(embeddings, offsets, limits):
    rows, depth = embeddings.shape
    count = lax.axis_size(AXES)
    assert count % 4 == 0 and lax.axis_size("sub") % 4 == 0
    tail = BAND - 2 * rows
    split = 2 * rows // 3
    assert 0 < tail <= rows and split % 16 == 0

    head, = copies_of(head_kernel, embeddings, [split], pltpu.SemaphoreType.DMA, "head")
    mate = shift(embeddings, count, to_core)
    rest, tail_rows = copies_of(
        parts_kernel, embeddings, [rows - split, tail], pltpu.SemaphoreType.DMA((2,)), "parts"
    )
    pair_head = shift(head, count, to_pair)
    far = shift(after(tail_rows, mate), count, to_far)
    row, column, positive, positive_row = index_of(
        limits, offsets[None], split, tail, 6 * rows + tail
    )

    windows, scores = [], []

    def score(blocks, state, last=False):
        low = sum(window.shape[0] for window in windows)
        window, score, state = scores_of(low, blocks, embeddings, column, row, positive_row, state, last)
        windows.append(window)
        scores.append(score)
        return state

    state = score([embeddings, mate], None)
    pair_rest = shift(after(rest, state[0]), count, to_pair)
    pair_mate_head = shift(after(pair_head, far, state[0]), count, to_core)
    cross_rest = shift(after(rest, pair_head, far), count, to_cross)
    cross_head = shift(after(pair_head, far, state[0]), count, to_next)
    pair_mate_rest = shift(pair_rest, count, to_core)
    state = score([far, pair_head, pair_mate_head, pair_rest, pair_mate_rest], state)
    cross_mate_rest = shift(cross_rest, count, to_core)
    cross_mate_head = shift(after(cross_head, state[0]), count, to_core)
    log_sum, note = score([cross_rest, cross_mate_rest, cross_head, cross_mate_head], state, True)

    mate_note = shift(note, count, to_core)
    pair_note = shift(note, count, to_pair)
    far_note = shift(note, count, to_far)
    cross_note = shift(pair_note, count, to_next)
    base = product_of(
        functools.partial(product_out_kernel, len(windows), split, tail),
        (*windows, *scores, column, positive, log_sum, row, note, mate_note, pair_note),
        [], VMEM, "product_out",
    )
    cross_note, far_note, base = lax.optimization_barrier((cross_note, far_note, base))
    other = shift(jnp.stack([pair_note, cross_note]), count, to_core)
    return product_of(
        functools.partial(product_back_kernel, len(windows) - 1, split, tail),
        (*windows[1:], *scores[1:], column, far_note, pair_note, cross_note, other, base),
        [pltpu.VMEM((rows, depth), jnp.float32), pltpu.SemaphoreType.DMA((depth // STEP,))],
        pl.BlockSpec(memory_space=pl.ANY), "product_back",
    )


def solution(mesh):
    return jax.shard_map(
        per_device,
        mesh=mesh,
        in_specs=(P(("videos", "tm", "sub"), None), P(("videos", "tm", "sub")), P("videos")),
        out_specs=P(("videos", "tm", "sub"), None),
        check_vma=False,
    )
```

```python
import functools

import jax
import jax.numpy as jnp
from jax import lax
from jax.experimental import pallas as pl
from jax.experimental.pallas import tpu as pltpu
from jax.sharding import PartitionSpec as P

BAND = 1024
SCALE = 16.0
AXES = ("tm", "sub")
NOWHERE = 1 << 29
LANES = 128
STEP = 512
VMEM = pl.BlockSpec(memory_space=pltpu.VMEM)
COST = pl.CostEstimate(flops=0, bytes_accessed=0, transcendentals=0)
PARAMS = pltpu.CompilerParams(vmem_limit_bytes=16 << 20)


def shift(x, count, target):
    pairs = [(i, target(i)) for i in range(count) if 0 <= target(i) < count]
    return lax.ppermute(x, AXES, pairs)


def after(x, *others):
    return lax.optimization_barrier((x, *others))[0]


def to_core(i):
    return i ^ 1


def to_pair(i):
    return i ^ 2


def to_cross(i):
    return i + 2 if i & 2 else i - 2


def to_next(i):
    return i - 4 if i & 2 else i + 4


def to_far(i):
    return i + 3 if i & 1 else i - 3


def is_second(axis_index, bit):
    return lax.rem(axis_index // bit, 2)


def head_kernel(own_ref, head_ref, sem):
    copy = pltpu.make_async_copy(own_ref.at[pl.ds(0, head_ref.shape[0])], head_ref, sem)
    copy.start()
    copy.wait()


def parts_kernel(own_ref, rest_ref, tail_ref, sems):
    rest, tail = rest_ref.shape[0], tail_ref.shape[0]
    core = is_second(lax.axis_index("sub"), 1)
    first = pl.multiple_of(core * (own_ref.shape[0] - tail), 16)
    copies = [
        pltpu.make_async_copy(own_ref.at[pl.ds(own_ref.shape[0] - rest, rest)], rest_ref, sems.at[0]),
        pltpu.make_async_copy(own_ref.at[pl.ds(first, tail)], tail_ref, sems.at[1]),
    ]
    for copy in copies:
        copy.start()
    for copy in copies:
        copy.wait()


def copies_of(kernel, own, sizes, semaphores, name):
    return pl.pallas_call(
        kernel,
        out_shape=[pltpu.VMEM((size, own.shape[1]), own.dtype) for size in sizes],
        in_specs=[pl.BlockSpec(memory_space=pl.ANY)],
        out_specs=[VMEM] * len(sizes),
        scratch_shapes=[semaphores],
        compiler_params=PARAMS,
        cost_estimate=COST,
        name=name,
    )(pltpu.with_memory_space_constraint(own, pltpu.HBM))


def index_kernel(split, tail, limits_ref, offset_ref, row_ref, column_ref, positive_ref, positive_row_ref):
    rows = offset_ref.shape[1]
    device = lax.axis_index("tm") * lax.axis_size("sub") + lax.axis_index("sub")
    core, chip = is_second(device, 1), is_second(device, 2)
    start, end = limits_ref[0], lax.axis_size(AXES) * rows - limits_ref[1]
    mate = device + 1 - 2 * core
    across, step = 2 - 4 * chip, 4 * chip - 2
    far = jnp.where(core == 1, (device + 3) * rows, (device - 2) * rows - tail)
    pair, pair_mate = (device + across) * rows, (mate + across) * rows
    cross, cross_mate = (device + step) * rows, (mate + step) * rows
    places = [
        (device * rows, rows), (mate * rows, rows), (far, tail),
        (pair, split), (pair_mate, split), (pair + split, rows - split), (pair_mate + split, rows - split),
        (cross + split, rows - split), (cross_mate + split, rows - split), (cross, split), (cross_mate, split),
    ]
    low = 0
    for base, size in places:
        index = base + lax.broadcasted_iota(jnp.int32, (1, size), 1)
        index = jnp.where((index >= start) & (index < end), index, NOWHERE)
        row_ref[:, low : low + size] = index.astype(jnp.float32)
        low += size
    index = device * rows + lax.broadcasted_iota(jnp.int32, (rows, 1), 0)
    index = jnp.where((index >= start) & (index < end), index, -NOWHERE)
    column_ref[...] = index.astype(jnp.float32)
    index = device * rows + lax.broadcasted_iota(jnp.int32, (1, rows), 1)
    forward = index + offset_ref[...]
    positive = jnp.where(forward < end, forward, index - offset_ref[...])
    positive = jnp.where((index >= start) & (index < end), positive, -1).astype(jnp.float32)
    positive_row_ref[...] = positive
    positive_ref[...] = jnp.broadcast_to(positive, (LANES, rows)).T[:, :1]


def index_of(limits, offsets, split, tail, width):
    rows = offsets.shape[1]
    shapes = [(1, width), (rows, 1), (rows, 1), (1, rows)]
    return pl.pallas_call(
        functools.partial(index_kernel, split, tail),
        out_shape=[jax.ShapeDtypeStruct(shape, jnp.float32) for shape in shapes],
        in_specs=[pl.BlockSpec(memory_space=pltpu.SMEM), VMEM],
        out_specs=[VMEM] * 4,
        compiler_params=PARAMS,
        cost_estimate=COST,
        name="index",
    )(limits, offsets)


def score_kernel(sizes, low, first, last, *refs):
    blocks = refs[: len(sizes)]
    column_ref, row_ref, positive_row_ref = refs[len(sizes) : len(sizes) + 3]
    refs = refs[len(sizes) + 3 :]
    if first:
        own = blocks[0][...]
    else:
        own = refs[0][...]
        old_peak, old_total = refs[1][:, :1], refs[2][:, :1]
        refs = refs[3:]
    window_ref, score_ref = refs[:2]
    rows = column_ref.shape[0]
    high = low + sum(sizes)
    block = jnp.concatenate([ref[...] for ref in blocks], axis=0)
    scores = SCALE * lax.dot_general(
        own, block, (((1,), (1,)), ((), ())), preferred_element_type=jnp.float32
    )
    spacing = column_ref[...] - row_ref[:, low:high]
    inside = jnp.abs(spacing) <= BAND
    if first:
        inside = inside & (spacing != 0.0)
    masked = jnp.where(inside, scores, -jnp.inf)
    score_ref[...] = masked
    peak = jnp.max(masked, axis=1, keepdims=True)
    if first:
        own_valid = column_ref[...] >= 0.0
        peak = jnp.where(own_valid, peak, 0.0)
    else:
        peak = jnp.maximum(peak, old_peak)
    total = jnp.sum(jnp.exp(score_ref[...] - peak), axis=1, keepdims=True)
    if first:
        total = total + jnp.where(own_valid, 0.0, 1.0)
    else:
        total = total + old_total * jnp.exp(old_peak - peak)
    window_ref[...] = block
    if last:
        log_ref, note_ref = refs[2:]
        log_sum = jnp.broadcast_to(peak + jnp.log(total), (rows, LANES))
        log_ref[...] = log_sum
        note_ref[:1] = log_sum.T[:1]
        note_ref[1:] = positive_row_ref[...]
    else:
        peak_ref, total_ref = refs[2:]
        peak_ref[...] = jnp.broadcast_to(peak, (rows, LANES))
        total_ref[...] = jnp.broadcast_to(total, (rows, LANES))


def scores_of(low, blocks, own, column, row, positive_row, state, last):
    rows, depth = own.shape
    sizes = tuple(block.shape[0] for block in blocks)
    width = sum(sizes)
    first = state is None
    wide = jax.ShapeDtypeStruct((rows, LANES), jnp.float32)
    shapes = [
        jax.ShapeDtypeStruct((width, depth), jnp.bfloat16),
        jax.ShapeDtypeStruct((rows, width), jnp.float32),
        wide,
        jax.ShapeDtypeStruct((2, rows), jnp.float32) if last else wide,
    ]
    operands = (*blocks, column, row, positive_row)
    if not first:
        operands = (*operands, own, *state)
    window, scores, *state = pl.pallas_call(
        functools.partial(score_kernel, sizes, low, first, last),
        out_shape=shapes,
        in_specs=[VMEM] * len(operands),
        out_specs=[VMEM] * len(shapes),
        compiler_params=PARAMS,
        cost_estimate=COST,
        name="scores_last" if last else ("scores_first" if first else "scores_next"),
    )(*operands)
    return window, scores, state


def weight_of(score, log_sum, index, wanted):
    weight = jnp.exp(score - log_sum) - jnp.where(index == wanted, 1.0, 0.0)
    return weight.astype(jnp.bfloat16)


def product_out_kernel(count, split, tail, *refs):
    windows, scores = refs[:count], refs[count : 2 * count]
    column_ref, positive_ref, log_ref, row_ref, own_note, mate_note, pair_note, out_ref = refs[2 * count :]
    log_sum, positive = log_ref[:, :1], positive_ref[...]
    weights = []
    low = 0
    for ref in scores:
        high = low + ref.shape[1]
        weights.append(weight_of(ref[...], log_sum, row_ref[:, low:high], positive))
        low = high
    notes = jnp.concatenate([own_note[...], mate_note[...]], axis=1)
    weights.append(weight_of(scores[0][...], notes[:1], notes[1:], column_ref[...]))
    weights.append(
        weight_of(scores[1][:, tail : tail + split], pair_note[:1, :split], pair_note[1:, :split], column_ref[...])
    )
    weights = jnp.concatenate(weights, axis=1)
    for low in range(0, out_ref.shape[1], STEP):
        place = slice(low, low + STEP)
        blocks = [ref[:, place] for ref in (*windows, windows[0])] + [windows[1][tail : tail + split, place]]
        block = jnp.concatenate(blocks, axis=0)
        out_ref[:, low : low + STEP] = jnp.dot(weights, block, preferred_element_type=jnp.float32)


def product_back_kernel(count, split, tail, *refs):
    windows, scores = refs[:count], refs[count : 2 * count]
    column_ref, far_note, pair_ref, cross_ref, other_ref, base_ref, out_ref, held_ref, sems = refs[2 * count :]
    rows = column_ref.shape[0]
    core = is_second(lax.axis_index("sub"), 1)
    pair, cross = pair_ref[...], cross_ref[...]
    pair_mate, cross_mate = other_ref[0], other_ref[1]
    far = jnp.where(core == 1, far_note[:, :tail], far_note[:, rows - tail :])
    notes = jnp.concatenate(
        [
            far, pair_mate[:, :split], pair[:, split:], pair_mate[:, split:],
            cross[:, split:], cross_mate[:, split:], cross[:, :split], cross_mate[:, :split],
        ],
        axis=1,
    )
    weights = []
    low = 0
    for number, ref in enumerate(scores):
        score = ref[...]
        if number == 0:
            score = jnp.concatenate([score[:, :tail], score[:, tail + split :]], axis=1)
        high = low + score.shape[1]
        weights.append(weight_of(score, notes[:1, low:high], notes[1:, low:high], column_ref[...]))
        low = high
    weights = jnp.concatenate(weights, axis=1)
    copies = []
    for number, low in enumerate(range(0, out_ref.shape[1], STEP)):
        place = pl.ds(low, STEP)
        first = windows[0][:, low : low + STEP]
        blocks = [first[:tail], first[tail + split :]] + [ref[:, low : low + STEP] for ref in windows[1:]]
        block = jnp.concatenate(blocks, axis=0)
        part = jnp.dot(weights, block, preferred_element_type=jnp.float32)
        held_ref[:, low : low + STEP] = SCALE * (part + base_ref[:, low : low + STEP])
        copies.append(pltpu.make_async_copy(held_ref.at[:, place], out_ref.at[:, place], sems.at[number]))
        copies[-1].start()
    for copy in copies:
        copy.wait()


def product_of(kernel, operands, scratch, place, name):
    rows, depth = operands[-1].shape if scratch else (operands[-1].shape[1], operands[0].shape[1])
    return pl.pallas_call(
        kernel,
        out_shape=jax.ShapeDtypeStruct((rows, depth), jnp.float32),
        in_specs=[VMEM] * len(operands),
        out_specs=place,
        scratch_shapes=scratch,
        compiler_params=PARAMS,
        cost_estimate=COST,
        name=name,
    )(*operands)


def per_device(embeddings, offsets, limits):
    rows, depth = embeddings.shape
    count = lax.axis_size(AXES)
    assert count % 4 == 0 and lax.axis_size("sub") % 4 == 0
    tail = BAND - 2 * rows
    split = 2 * rows // 3
    assert 0 < tail <= rows and split % 16 == 0

    head, = copies_of(head_kernel, embeddings, [split], pltpu.SemaphoreType.DMA, "head")
    mate = shift(embeddings, count, to_core)
    rest, tail_rows = copies_of(
        parts_kernel, embeddings, [rows - split, tail], pltpu.SemaphoreType.DMA((2,)), "parts"
    )
    pair_head = shift(head, count, to_pair)
    far = shift(after(tail_rows, mate), count, to_far)
    row, column, positive, positive_row = index_of(
        limits, offsets[None], split, tail, 6 * rows + tail
    )

    windows, scores = [], []

    def score(blocks, state, last=False):
        low = sum(window.shape[0] for window in windows)
        window, score, state = scores_of(low, blocks, embeddings, column, row, positive_row, state, last)
        windows.append(window)
        scores.append(score)
        return state

    state = score([embeddings, mate], None)
    pair_rest = shift(after(rest, state[0]), count, to_pair)
    pair_mate_head = shift(after(pair_head, far, state[0]), count, to_core)
    cross_rest = shift(after(rest, pair_head, far), count, to_cross)
    cross_head = shift(after(pair_head, far, state[0]), count, to_next)
    pair_mate_rest = shift(pair_rest, count, to_core)
    state = score([far, pair_head, pair_mate_head, pair_rest, pair_mate_rest], state)
    cross_mate_rest = shift(cross_rest, count, to_core)
    cross_mate_head = shift(after(cross_head, state[0]), count, to_core)
    log_sum, note = score([cross_rest, cross_mate_rest, cross_head, cross_mate_head], state, True)

    mate_note = shift(note, count, to_core)
    pair_note = shift(note, count, to_pair)
    far_note = shift(note, count, to_far)
    cross_note = shift(pair_note, count, to_next)
    base = product_of(
        functools.partial(product_out_kernel, len(windows), split, tail),
        (*windows, *scores, column, positive, log_sum, row, note, mate_note, pair_note),
        [], VMEM, "product_out",
    )
    cross_note, far_note, base = lax.optimization_barrier((cross_note, far_note, base))
    other = shift(jnp.stack([pair_note, cross_note]), count, to_core)
    return product_of(
        functools.partial(product_back_kernel, len(windows) - 1, split, tail),
        (*windows[1:], *scores[1:], column, far_note, pair_note, cross_note, other, base),
        [pltpu.VMEM((rows, depth), jnp.float32), pltpu.SemaphoreType.DMA((depth // STEP,))],
        pl.BlockSpec(memory_space=pl.ANY), "product_back",
    )


def solution(mesh):
    return jax.shard_map(
        per_device,
        mesh=mesh,
        in_specs=(P(("videos", "tm", "sub"), None), P(("videos", "tm", "sub")), P("videos")),
        out_specs=P(("videos", "tm", "sub"), None),
        check_vma=False,
    )
```
